32 devices in a mesh: groups: 2 (over y), seq: 4 (over z), blk: 2 (over x), cfg: 2 (over core).
Axes of the slice: x: 2, y: 2, z: 4, core: 2. Of those that a mesh axis runs over, the one named last changes fastest.
Arguments:
- queries: bfloat16 [4, 320, 4096], P(('groups', 'cfg'), ('seq', 'blk')), parts along dimension 0, may hold values from -6 to 6
- keys: bfloat16 [4, 320, 4096], P(('groups', 'cfg'), ('seq', 'blk')), parts along dimension 0, may hold values from -6 to 6
- values: bfloat16 [4, 320, 4096], P(('groups', 'cfg'), ('seq', 'blk')), parts along dimension 0, may hold values from -6 to 6
- ref_keys: bfloat16 [4, 1024, 4096], P(('groups', 'cfg'), 'seq'), parts along dimension 0, may hold values from -6 to 6
- ref_values: bfloat16 [4, 1024, 4096], P(('groups', 'cfg'), 'seq'), parts along dimension 0, may hold values from -6 to 6
- ref_len: int32 [4], P(('groups', 'cfg')), parts along dimension 0, may hold values from 256 to 1024, as said below
- step_index: int32 [2], P('groups'), parts along dimension 0, may hold values from 0 to 49
- guide: float32 [2], P('groups'), parts along dimension 0, may hold values from 3 to 6
- latent: float32 [320, 128], P(('groups', 'seq', 'blk', 'cfg')), parts along dimension 0, may hold values from -6 to 6
- w_out: bfloat16 [4096, 64], replicated, may hold values from -1 to 1
Outputs:
- latent_next: float32 [320, 128], P(('groups', 'seq', 'blk', 'cfg')), parts along dimension 0
- denoised: float32 [320, 128], P(('groups', 'seq', 'blk', 'cfg')), parts along dimension 0
The draws below stay inside these ranges and needn't reach their ends.
There are 2 independent parts, one for each index of `groups`. The reference program is written for one: setup_inputs(seed, part) draws one part's arguments, and reference() takes and returns one part's arrays. A program takes and returns all parts, laid end to end along the dimension named above; an argument that names none is the same for every part. Nothing has to cross between parts.
Inputs may be any that keep to these rules, and one draw needn't show every extreme that they name: `ref_len`: one of the two branches has exactly 1024 valid reference tokens.
All inputs are finite; a program needn't handle non-finite values.
Results may differ from the reference program's by a relative error of at most 0.005.
Values may be sent and summed in bfloat16 or wider, within the bound.
A program may use at most 128 MiB of HBM per device.

```python
import jax
import jax.numpy as jnp
from jax import lax

HEADS = 32
HD = 128
C_OUT = 64
STEPS = 50
REF = 1024
TOKENS = 320


def drawn_base(key, rows):
    width = HEADS * HD
    return jnp.clip(jax.random.normal(jax.random.fold_in(key, 1), (2, rows, width), jnp.float32), -5.0, 5.0)


def draw_queries(key, part):
    own = jax.random.fold_in(key, 101)
    result = drawn_base(own, TOKENS)
    return result.astype(jnp.bfloat16)


def draw_keys(key, part):
    own = jax.random.fold_in(key, 202)
    result = drawn_base(own, TOKENS)
    return result.astype(jnp.bfloat16)


def draw_ref_keys(key, part):
    own = jax.random.fold_in(key, 303)
    result = drawn_base(own, REF)
    return result.astype(jnp.bfloat16)


def draw_ref_len(key, part):
    which = jax.random.randint(jax.random.fold_in(key, 401), (), 0, 2)
    other = jax.random.randint(jax.random.fold_in(key, 402), (), REF // 4, REF + 1)
    return jnp.where(jnp.arange(2) == which, REF, other).astype(jnp.int32)


def steps_of(rng, extent, cuts, low, top_value):
    factor_of = 1.0
    for position, shards_of in cuts:
        steps = jax.random.uniform(jax.random.fold_in(jax.random.fold_in(rng, 6), position), (shards_of,), jnp.float32, low / len(cuts), top_value / len(cuts))
        factor_of = factor_of * jnp.repeat(jnp.exp(steps), extent[position] // shards_of).reshape((-1,) + (1,) * (len(extent) - 1 - position))
    return factor_of


def normal_values(key, shape, scale, bound, cuts=(), kind=jnp.bfloat16):
    loudness = steps_of(key, shape, cuts, -0.22, 0.18) if cuts else 1.0
    values = jax.random.normal(key, shape, jnp.float32) * scale * loudness
    return jnp.minimum(jnp.maximum(values, -bound), bound).astype(kind)


def setup_inputs(seed: int = 0, part: int = 0) -> dict:
    arg_keys = jax.random.split(jax.random.key(seed), 11)
    part_splits = jax.random.split(jax.random.fold_in(arg_keys[10], part), 11)
    queries = draw_queries(jax.random.fold_in(jax.random.fold_in(arg_keys[10], part), 71), part)
    keys = draw_keys(jax.random.fold_in(jax.random.fold_in(arg_keys[10], part), 71), part)
    values = normal_values(part_splits[2], (2, TOKENS, HEADS * HD), 1.0, 6.0, ((0, 2), (1, 8)))
    ref_keys = draw_ref_keys(jax.random.fold_in(jax.random.fold_in(arg_keys[10], part), 71), part)
    ref_values = normal_values(part_splits[4], (2, REF, HEADS * HD), 1.0, 6.0, ((0, 2), (1, 4)))
    ref_len = draw_ref_len(jax.random.fold_in(jax.random.fold_in(arg_keys[10], part), 71), part)
    step_index = jax.random.randint(part_splits[6], (1,), 0, STEPS).astype(jnp.int32)
    guide = jnp.clip(jax.random.uniform(part_splits[7], (1,), jnp.float32, 3.0, 6.0), 3.0, 6.0)
    latent = normal_values(part_splits[8], (TOKENS // 2, 2 * C_OUT), 1.0, 6.0, ((0, 16),), jnp.float32)
    w_out = normal_values(arg_keys[9], (HEADS * HD, C_OUT), (0.3 * (HEADS * HD) ** -0.5 * (TOKENS * REF * (TOKENS + REF) ** -1) ** 0.5), 1.0)
    return dict(queries=queries, keys=keys, values=values, ref_keys=ref_keys, ref_values=ref_values, ref_len=ref_len, step_index=step_index, guide=guide, latent=latent, w_out=w_out)


def head_attention(packed, length):
    query_head, key_head, value_head, refkey_head, refvalue_head = packed
    scale_factor = HD ** -0.5
    scores = jnp.dot(query_head, key_head.T, preferred_element_type=jnp.float32) * scale_factor
    top_score = jnp.max(scores, axis=1, keepdims=True)
    weights = jnp.exp(scores - top_score)
    self_out = jnp.dot(weights.astype(jnp.bfloat16), value_head, preferred_element_type=jnp.float32) / jnp.sum(weights, axis=1, keepdims=True)
    ref_scores = jnp.dot(query_head, refkey_head.T, preferred_element_type=jnp.float32) * scale_factor
    ref_index = jnp.arange(ref_scores.shape[1], dtype=jnp.int32)[None, :]
    ref_scores = jnp.where(ref_index < length, ref_scores, jnp.float32(-1e30))
    ref_top = jnp.max(ref_scores, axis=1, keepdims=True)
    ref_weights = jnp.exp(ref_scores - ref_top)
    ref_out = jnp.dot(ref_weights.astype(jnp.bfloat16), refvalue_head, preferred_element_type=jnp.float32) / jnp.sum(ref_weights, axis=1, keepdims=True)
    return self_out + ref_out


def branch_velocity(query_rows, key_rows, value_rows, refkey_rows, refvalue_rows, length, w_out):
    def split_heads(array):
        return array.reshape(array.shape[0], HEADS, HD).transpose(1, 0, 2)

    packed = (split_heads(query_rows), split_heads(key_rows), split_heads(value_rows), split_heads(refkey_rows), split_heads(refvalue_rows))
    outputs = lax.map(lambda item: head_attention(item, length), packed)
    attended = outputs.transpose(1, 0, 2).reshape(TOKENS, HEADS * HD).astype(jnp.bfloat16)
    velocity = jnp.dot(attended, w_out, preferred_element_type=jnp.float32)
    return velocity.reshape(TOKENS // 2, 2 * C_OUT)


def sigma_of(index):
    frac = 1.0 - index.astype(jnp.float32) / STEPS
    return 5.0 * frac / (1.0 + 4.0 * frac)


def reference(queries, keys, values, ref_keys, ref_values, ref_len, step_index, guide, latent, w_out):
    cond_vel = branch_velocity(queries[0], keys[0], values[0], ref_keys[0], ref_values[0], ref_len[0], w_out)
    uncond_vel = branch_velocity(queries[1], keys[1], values[1], ref_keys[1], ref_values[1], ref_len[1], w_out)
    guided = uncond_vel + guide[0] * (cond_vel - uncond_vel)
    sig_now = sigma_of(step_index[0])
    sig_next = sigma_of(step_index[0] + 1)
    latent_next = latent + (sig_next - sig_now) * guided
    denoised = latent - sig_now * guided
    return latent_next, denoised
```

```python
import functools
import math

import jax
import jax.numpy as jnp
from jax import lax
from jax.experimental import pallas as pl
from jax.experimental.pallas import tpu as pltpu
from jax.sharding import PartitionSpec as P

HD = 128
STEPS = 50
FACTOR = HD ** (-0.5) * math.log2(math.e)
MESH = pl.DeviceIdType.MESH
BF16 = jnp.bfloat16
F32 = jnp.float32


def round_up(value, unit):
    return (value + unit - 1) // unit * unit


def sigma_of(frac_index):
    frac = 1.0 - frac_index / STEPS
    return 5.0 * frac / (1.0 + 4.0 * frac)


def dot_t(a, b):
    return lax.dot_general(a, b, (((1,), (1,)), ((), ())), preferred_element_type=F32)


def step_kernel(
    n,
    nx,
    nc,
    len_ref,
    step_ref,
    guide_ref,
    q_ref,
    k_ref,
    v_ref,
    rk_ref,
    rv_ref,
    w_ref,
    latent_ref,
    next_ref,
    denoised_ref,
    qbuf,
    kbuf,
    vbuf,
    rkey,
    rval,
    wraw,
    wdup,
    kself,
    vself,
    oref,
    oself,
    mstat,
    lstat,
    lse,
    att,
    vtmp,
    slab,
    landed,
    local_sem,
    x_send,
    q_recv,
    kv_recv,
    z_send,
    s_send,
    s_recv,
    v_send,
    v_recv,
):
    z = lax.axis_index("seq")
    x = lax.axis_index("blk")
    c = lax.axis_index("cfg")
    rows = q_ref.shape[1]
    width = qbuf.shape[3]
    heads = width // HD
    block = nx * rows
    padded = lse.shape[3]
    lanes_used = lse.shape[2]
    half = latent_ref.shape[0]
    refs = rkey.shape[0]

    def cols(index):
        return pl.ds(pl.multiple_of(index * width, HD), width)

    loads = [
        pltpu.make_async_copy(q_ref.at[0, :, cols(x)], qbuf.at[z, x], local_sem.at[0]),
        pltpu.make_async_copy(rk_ref.at[0, :, cols(x)], rkey, local_sem.at[1]),
        pltpu.make_async_copy(rv_ref.at[0, :, cols(x)], rval, local_sem.at[2]),
        pltpu.make_async_copy(k_ref.at[0, :, cols(x)], kbuf.at[x], local_sem.at[3]),
        pltpu.make_async_copy(v_ref.at[0, :, cols(x)], vbuf.at[x], local_sem.at[4]),
        pltpu.make_async_copy(
            w_ref.at[pl.ds(pl.multiple_of(x * width, HD), width), :], wraw, local_sem.at[5]
        ),
    ]
    for load in loads:
        load.start()

    members = n * nx * nc
    me = (z * nx + x) * nc + c

    def coords(index):
        return {"seq": index // (nx * nc), "blk": (index // nc) % nx, "cfg": index % nc}

    barrier = pltpu.get_barrier_semaphore()

    def greet(offset, carry):
        pl.semaphore_signal(
            barrier, inc=1, device_id=coords((me + offset) % members), device_id_type=MESH
        )
        return carry

    lax.fori_loop(1, members, greet, 0)
    pl.semaphore_wait(barrier, members - 1)

    def x_copy(offset, kind):
        source = (q_ref, k_ref, v_ref)[kind]
        target = (qbuf.at[z, x], kbuf.at[x], vbuf.at[x])[kind]
        arrived = (q_recv.at[z, x], kv_recv.at[0, x], kv_recv.at[1, x])[kind]
        to = (x + offset) % nx
        return pltpu.make_async_remote_copy(
            src_ref=source.at[0, :, cols(to)],
            dst_ref=target,
            send_sem=x_send.at[kind, offset],
            recv_sem=arrived,
            device_id={"blk": to},
            device_id_type=MESH,
        )

    def z_copy(side, b, piece):
        return pltpu.make_async_remote_copy(
            src_ref=qbuf.at[b, piece],
            dst_ref=qbuf.at[b, piece],
            send_sem=z_send.at[side, b, piece],
            recv_sem=q_recv.at[b, piece],
            device_id={"seq": z + 1 - 2 * side},
            device_id_type=MESH,
        )

    def forward(side, b, piece):
        @pl.when((z < n - 1) if side == 0 else (z > 0))
        def _():
            z_copy(side, b, piece).start()

    def arrived_q(b, piece):
        pltpu.make_async_remote_copy(
            src_ref=qbuf.at[b, piece],
            dst_ref=qbuf.at[b, piece],
            send_sem=z_send.at[0, b, piece],
            recv_sem=q_recv.at[b, piece],
            device_id={"blk": (x + 1) % nx},
            device_id_type=MESH,
        ).wait_recv()

    for kind in range(3):
        for offset in range(1, nx):
            x_copy(offset, kind).start()
    loads[0].wait()
    forward(0, z, x)
    forward(1, z, x)
    for offset in range(1, nx):
        piece = (x + offset) % nx
        arrived_q(z, piece)
        forward(0, z, piece)
        forward(1, z, piece)

    loads[5].wait()
    weight = wraw[...]
    wdup[...] = jnp.concatenate([weight, weight], axis=1)
    loads[1].wait()
    loads[2].wait()

    ref_index = lax.broadcasted_iota(jnp.int32, (1, refs), 1) + z * refs
    bias = jnp.where(ref_index < len_ref[0], jnp.float32(0.0), jnp.float32(-1e30))
    lane = lax.broadcasted_iota(jnp.int32, (block, HD), 1)

    def joined(ref, index, h):
        span = pl.ds(h * HD, HD)
        parts = [ref[index + (p, slice(None), span)].astype(F32) for p in range(nx)]
        return (jnp.concatenate(parts, axis=0) if nx > 1 else parts[0]).astype(BF16)

    def attend(b, h, key_rows, value_rows, bias_row):
        scores = dot_t(joined(qbuf, (b,), h), key_rows)
        if bias_row is not None:
            scores = scores + bias_row
        top = jnp.max(scores, axis=1, keepdims=True)
        weights = jnp.exp2((scores - top) * FACTOR).astype(BF16)
        ones = jnp.ones(value_rows.shape, BF16)
        summed = jnp.dot(
            weights, jnp.concatenate([value_rows, ones], axis=1), preferred_element_type=F32
        )
        return top, summed[:, :HD], summed[:, HD:]

    def ref_part(b):
        tops = jnp.zeros((block, HD), F32)
        totals = jnp.ones((block, HD), F32)
        for h in range(heads):
            span = pl.ds(h * HD, HD)
            top, summed, total = attend(b, h, rkey[:, span], rval[:, span], bias)
            oref[b, :, span] = summed
            tops = jnp.where(lane == h, top, tops)
            totals = jnp.where(lane == h, total, totals)
        mstat[b, pl.ds(0, block), :] = tops
        lstat[b, pl.ds(0, block), :] = totals

    def lse_copy(b, offset):
        to = (z + offset) % n
        return pltpu.make_async_remote_copy(
            src_ref=lse.at[z, b],
            dst_ref=lse.at[z, b],
            send_sem=s_send.at[offset, b],
            recv_sem=s_recv.at[z, b],
            device_id={"seq": to},
            device_id_type=MESH,
        )

    def self_part(b):
        tops = mstat[b, pl.ds(0, block), :]
        totals = lstat[b, pl.ds(0, block), :]
        for h in range(heads):
            span = pl.ds(h * HD, HD)
            top, summed, total = attend(b, h, kself[:, span], vself[:, span], None)
            oself[b, :, span] = summed
            tops = jnp.where(lane == heads + h, top, tops)
            totals = jnp.where(lane == heads + h, total, totals)
        tops = tops * FACTOR
        mstat[b, pl.ds(0, block), :] = tops
        lstat[b, pl.ds(0, block), :] = tops + jnp.log2(totals)
        for start in range(0, padded, HD):
            turned = lstat[b, pl.ds(start, HD), :].T
            lse[z, b, :, pl.ds(start, HD)] = turned[:lanes_used, :]
        for offset in range(1, n):
            lse_copy(b, offset).start()

    def receive_step(s):
        for side in range(2):
            b = z - s if side == 0 else z + s

            @pl.when((b >= 0) if side == 0 else (b < n))
            def _():
                for piece in range(nx):
                    arrived_q(b, piece)
                    forward(side, b, piece)

    def each_side(s, work):
        def one(side, carry):
            b = z + s * (2 * side - 1)

            @pl.when((b >= 0) & (b < n))
            def _():
                work(b)

            return carry

        lax.fori_loop(0, 2, one, 0)

    def block_of(j):
        return z + ((j + 1) // 2) * (1 - 2 * (j % 2))

    def visit(j, carry):
        b = block_of(j)

        @pl.when((j % 2 == 1))
        def _():
            receive_step((j + 1) // 2)

        @pl.when((b >= 0) & (b < n))
        def _():
            ref_part(b)

        @pl.when(j == min(2, 2 * n - 2))
        def _():
            loads[3].wait()
            loads[4].wait()
            for offset in range(1, nx):
                for kind in (1, 2):
                    other = (x + offset) % nx
                    target = (kbuf, vbuf)[kind - 1].at[other]
                    pltpu.make_async_remote_copy(
                        src_ref=target,
                        dst_ref=target,
                        send_sem=x_send.at[kind, offset],
                        recv_sem=kv_recv.at[kind - 1, other],
                        device_id={"blk": other},
                        device_id_type=MESH,
                    ).wait_recv()
            for h in range(heads):
                span = pl.ds(h * HD, HD)
                kself[:, span] = joined(kbuf, (), h)
                vself[:, span] = joined(vbuf, (), h)

        low = jnp.where(j == 2, 0, j) if n > 1 else j
        high = jnp.where(j < min(2, 2 * n - 2), low, j + 1)

        def late(i, inner):
            d = block_of(i)

            @pl.when((d >= 0) & (d < n))
            def _():
                self_part(d)

            return inner

        lax.fori_loop(low, high, late, 0)
        return carry

    lax.fori_loop(0, 2 * n - 1, visit, 0)

    gain = jnp.where(c == 0, guide_ref[0], 1.0 - guide_ref[0])
    half_lane = lax.broadcasted_iota(jnp.int32, (half, HD), 1)

    def slab_copy(index):
        return pltpu.make_async_remote_copy(
            src_ref=slab.at[index],
            dst_ref=landed.at[me],
            send_sem=v_send.at[index],
            recv_sem=v_recv.at[me],
            device_id=coords(index),
            device_id_type=MESH,
        )

    def project(i, carry):
        b = (i + 1) % n
        for offset in range(1, n):
            source = (z + offset) % n
            pltpu.make_async_remote_copy(
                src_ref=lse.at[source, b],
                dst_ref=lse.at[source, b],
                send_sem=s_send.at[offset, b],
                recv_sem=s_recv.at[source, b],
                device_id={"seq": source},
                device_id_type=MESH,
            ).wait_recv()
        for start in range(0, padded, HD):
            span = pl.ds(start, HD)
            parts = [lse[source, b, :, span] for source in range(n)]
            top = functools.reduce(jnp.maximum, parts)
            total = sum(jnp.exp2(part - top) for part in parts)
            whole = top + jnp.log2(total)
            pad = jnp.zeros((HD - lanes_used, HD), F32)
            lstat[b, span, :] = jnp.concatenate([whole, pad], axis=0).T
        share = jnp.exp2(mstat[b, pl.ds(0, block), :] - lstat[b, pl.ds(0, block), :])
        for h in range(heads):
            span = pl.ds(h * HD, HD)
            mixed = (
                share[:, h : h + 1] * oref[b, :, span]
                + share[:, heads + h : heads + h + 1] * oself[b, :, span]
            )
            att[:, span] = mixed.astype(BF16)
        vtmp[...] = gain * jnp.dot(att[...], wdup[...], preferred_element_type=F32)
        for other in range(nx):
            for branch in range(nc):
                first = other * rows + branch * 2 * half
                even = vtmp[pl.ds(first, half, stride=2), :]
                odd = vtmp[pl.ds(first + 1, half, stride=2), :]
                value = jnp.where(half_lane < HD // 2, even, odd)
                index = (b * nx + other) * nc + branch
                slab[index, pl.ds(0, half), :] = value

                @pl.when(index != me)
                def _():
                    slab_copy(index).start()

                @pl.when(index == me)
                def _():
                    landed[index, pl.ds(0, half), :] = value

        return carry

    lax.fori_loop(0, n, project, 0)

    for kind in range(3):
        for offset in range(1, nx):
            x_copy(offset, kind).wait_send()

    def sent(b, carry):
        for piece in range(nx):

            @pl.when((z < n - 1) & (b <= z))
            def _():
                z_copy(0, b, piece).wait_send()

            @pl.when((z > 0) & (b >= z))
            def _():
                z_copy(1, b, piece).wait_send()

        for offset in range(1, n):
            lse_copy(b, offset).wait_send()
        return carry

    lax.fori_loop(0, n, sent, 0)

    def collect(offset, carry):
        source = (me + offset) % members
        pltpu.make_async_remote_copy(
            src_ref=slab.at[source],
            dst_ref=landed.at[source],
            send_sem=v_send.at[source],
            recv_sem=v_recv.at[source],
            device_id=coords(source),
            device_id_type=MESH,
        ).wait()
        return carry

    lax.fori_loop(1, members, collect, 0)

    guided = jnp.sum(landed[:, pl.ds(0, half), :], axis=0)
    now = jnp.full((half, HD), step_ref[0], jnp.int32)
    sig_now = sigma_of(now.astype(F32))
    sig_next = sigma_of((now + 1).astype(F32))
    latent = latent_ref[...]
    next_ref[...] = latent + (sig_next - sig_now) * guided
    denoised_ref[...] = latent - sig_now * guided


def on_device(
    n,
    nx,
    nc,
    queries,
    keys,
    values,
    ref_keys,
    ref_values,
    ref_len,
    step_index,
    guide,
    latent,
    w_out,
):
    rows, wide = queries.shape[1:]
    refs = ref_keys.shape[1]
    width = wide // nx
    heads = width // HD
    block = nx * rows
    padded = round_up(block, HD)
    lanes_used = round_up(2 * heads, 8)
    members = n * nx * nc
    half = latent.shape[0]
    out = jax.ShapeDtypeStruct(latent.shape, F32)
    smem = pl.BlockSpec(memory_space=pltpu.SMEM)
    vmem = pl.BlockSpec(memory_space=pltpu.VMEM)
    anywhere = pl.BlockSpec(memory_space=pl.ANY)
    dma = pltpu.SemaphoreType.DMA
    flops = 4 * n * block * heads * HD * (refs + block)
    return pl.pallas_call(
        functools.partial(step_kernel, n, nx, nc),
        out_shape=(out, out),
        in_specs=[smem] * 3 + [anywhere] * 6 + [vmem],
        out_specs=(vmem, vmem),
        scratch_shapes=[
            pltpu.VMEM((n, nx, rows, width), BF16),
            pltpu.VMEM((nx, rows, width), BF16),
            pltpu.VMEM((nx, rows, width), BF16),
            pltpu.VMEM((refs, width), BF16),
            pltpu.VMEM((refs, width), BF16),
            pltpu.VMEM((width, w_out.shape[1]), BF16),
            pltpu.VMEM((width, 2 * w_out.shape[1]), BF16),
            pltpu.VMEM((block, width), BF16),
            pltpu.VMEM((block, width), BF16),
            pltpu.VMEM((n, block, width), F32),
            pltpu.VMEM((n, block, width), F32),
            pltpu.VMEM((n, padded, HD), F32),
            pltpu.VMEM((n, padded, HD), F32),
            pltpu.VMEM((n, n, lanes_used, padded), F32),
            pltpu.VMEM((block, width), BF16),
            pltpu.VMEM((block, HD), F32),
            pltpu.VMEM((members, round_up(half, 8), HD), F32),
            pltpu.VMEM((members, round_up(half, 8), HD), F32),
            dma((6,)),
            dma((3, nx)),
            dma((n, nx)),
            dma((2, nx)),
            dma((2, n, nx)),
            dma((n, n)),
            dma((n, n)),
            dma((members,)),
            dma((members,)),
        ],
        compiler_params=pltpu.CompilerParams(
            collective_id=0, has_side_effects=True, vmem_limit_bytes=58 * 2**20
        ),
        cost_estimate=pl.CostEstimate(
            flops=flops, bytes_accessed=4 * refs * width * 2, transcendentals=0
        ),
    )(ref_len, step_index, guide, queries, keys, values, ref_keys, ref_values, w_out, latent)


def solution(mesh):
    in_specs = (
        P(("groups", "cfg"), ("seq", "blk"), None),
        P(("groups", "cfg"), ("seq", "blk"), None),
        P(("groups", "cfg"), ("seq", "blk"), None),
        P(("groups", "cfg"), "seq", None),
        P(("groups", "cfg"), "seq", None),
        P(("groups", "cfg")),
        P("groups"),
        P("groups"),
        P(("groups", "seq", "blk", "cfg"), None),
        P(),
    )
    out_specs = (P(("groups", "seq", "blk", "cfg"), None), P(("groups", "seq", "blk", "cfg"), None))
    body = functools.partial(on_device, mesh.shape["seq"], mesh.shape["blk"], mesh.shape["cfg"])
    return jax.shard_map(
        body, mesh=mesh, in_specs=in_specs, out_specs=out_specs, check_vma=False
    )
```

```python
import functools
import math

import jax
import jax.numpy as jnp
from jax import lax
from jax.experimental import pallas as pl
from jax.experimental.pallas import tpu as pltpu
from jax.sharding import PartitionSpec as P

HD = 128
STEPS = 50
FACTOR = HD ** (-0.5) * math.log2(math.e)
MESH = pl.DeviceIdType.MESH
BF16 = jnp.bfloat16
F32 = jnp.float32


def round_up(value, unit):
    return (value + unit - 1) // unit * unit


def sigma_of(frac_index):
    frac = 1.0 - frac_index / STEPS
    return 5.0 * frac / (1.0 + 4.0 * frac)


def dot_t(a, b):
    return lax.dot_general(a, b, (((1,), (1,)), ((), ())), preferred_element_type=F32)


def step_kernel(
    n,
    nx,
    nc,
    chunks,
    len_ref,
    step_ref,
    guide_ref,
    q_ref,
    k_ref,
    v_ref,
    rk_ref,
    rv_ref,
    w_ref,
    delta_ref,
    qbuf,
    kbuf,
    vbuf,
    rkey,
    rval,
    wdup,
    kself,
    vself,
    oref,
    oself,
    mstat,
    lstat,
    lse,
    att,
    vtmp,
    slab,
    landed,
    local_sem,
    x_send,
    kv_send,
    q_recv,
    kv_recv,
    z_send,
    s_send,
    s_recv,
    v_send,
    v_recv,
):
    z = lax.axis_index("seq")
    x = lax.axis_index("blk")
    c = lax.axis_index("cfg")
    rows = q_ref.shape[1]
    width = qbuf.shape[3]
    heads = width // HD
    per = heads // chunks
    part = per * HD
    block = nx * rows
    padded = lse.shape[3]
    lanes_used = lse.shape[2]
    half = delta_ref.shape[1]
    refs = rkey.shape[0]
    outs = w_ref.shape[0]
    late = min(2, max(1, n - 2))

    def cols(index):
        return pl.ds(pl.multiple_of(index * width, HD), width)

    def chunk(ch):
        return pl.ds(pl.multiple_of(ch * part, HD), part)

    loads = [
        pltpu.make_async_copy(q_ref.at[0, :, cols(x)], qbuf.at[z, x], local_sem.at[0]),
        pltpu.make_async_copy(rk_ref.at[0, :, cols(x)], rkey, local_sem.at[1]),
        pltpu.make_async_copy(rv_ref.at[0, :, cols(x)], rval, local_sem.at[2]),
        pltpu.make_async_copy(k_ref.at[0, :, cols(x)], kbuf.at[x], local_sem.at[3]),
        pltpu.make_async_copy(v_ref.at[0, :, cols(x)], vbuf.at[x], local_sem.at[4]),
        pltpu.make_async_copy(w_ref.at[:, cols(x)], wdup.at[pl.ds(0, outs)], local_sem.at[5]),
        pltpu.make_async_copy(w_ref.at[:, cols(x)], wdup.at[pl.ds(outs, outs)], local_sem.at[6]),
    ]
    for load in loads:
        load.start()

    members = n * nx * nc
    me = (z * nx + x) * nc + c

    def coords(index):
        return {"seq": index // (nx * nc), "blk": (index // nc) % nx, "cfg": index % nc}

    barrier = pltpu.get_barrier_semaphore()

    def greet(offset, carry):
        pl.semaphore_signal(
            barrier, inc=1, device_id=coords((me + offset) % members), device_id_type=MESH
        )
        return carry

    lax.fori_loop(1, members, greet, 0)
    pl.semaphore_wait(barrier, members - 1)

    def xq_copy(offset, ch):
        to = (x + offset) % nx
        span = pl.ds(pl.multiple_of(to * width + ch * part, HD), part)
        return pltpu.make_async_remote_copy(
            src_ref=q_ref.at[0, :, span],
            dst_ref=qbuf.at[z, x, :, chunk(ch)],
            send_sem=x_send.at[offset, ch],
            recv_sem=q_recv.at[z, x, ch],
            device_id={"blk": to},
            device_id_type=MESH,
        )

    def xkv_copy(offset, kind):
        to = (x + offset) % nx
        return pltpu.make_async_remote_copy(
            src_ref=(k_ref, v_ref)[kind].at[0, :, cols(to)],
            dst_ref=(kbuf, vbuf)[kind].at[x],
            send_sem=kv_send.at[kind, offset],
            recv_sem=kv_recv.at[kind, x],
            device_id={"blk": to},
            device_id_type=MESH,
        )

    def z_copy(side, b, piece, ch):
        ref = qbuf.at[b, piece, :, chunk(ch)]
        return pltpu.make_async_remote_copy(
            src_ref=ref,
            dst_ref=ref,
            send_sem=z_send.at[side, b, piece, ch],
            recv_sem=q_recv.at[b, piece, ch],
            device_id={"seq": z + 1 - 2 * side},
            device_id_type=MESH,
        )

    def forward(side, b, piece, ch):
        @pl.when((z < n - 1) if side == 0 else (z > 0))
        def _():
            z_copy(side, b, piece, ch).start()

    def arrived_q(b, piece, ch):
        ref = qbuf.at[b, piece, :, chunk(ch)]
        pltpu.make_async_remote_copy(
            src_ref=ref,
            dst_ref=ref,
            send_sem=z_send.at[0, b, piece, ch],
            recv_sem=q_recv.at[b, piece, ch],
            device_id={"blk": (x + 1) % nx},
            device_id_type=MESH,
        ).wait_recv()

    for ch in range(chunks):
        for offset in range(1, nx):
            xq_copy(offset, ch).start()
    loads[0].wait()
    for ch in range(chunks):
        forward(0, z, x, ch)
        forward(1, z, x, ch)
    for ch in range(chunks):
        for offset in range(1, nx):
            piece = (x + offset) % nx
            arrived_q(z, piece, ch)
            forward(0, z, piece, ch)
            forward(1, z, piece, ch)
    for kind in range(2):
        for offset in range(1, nx):
            xkv_copy(offset, kind).start()
    for load in loads[1:3] + loads[5:]:
        load.wait()

    ref_index = lax.broadcasted_iota(jnp.int32, (1, refs), 1) + z * refs
    bias = jnp.where(ref_index < len_ref[0], jnp.float32(0.0), jnp.float32(-1e30))
    lane = lax.broadcasted_iota(jnp.int32, (block, HD), 1)

    def joined(ref, index, span):
        parts = [ref[index + (p, slice(None), span)].astype(F32) for p in range(nx)]
        return (jnp.concatenate(parts, axis=0) if nx > 1 else parts[0]).astype(BF16)

    def attend(b, ch, with_ref, with_self):
        tops = mstat[b, pl.ds(0, block), :]
        totals = lstat[b, pl.ds(0, block), :]
        spans = [pl.ds(pl.multiple_of(ch * part + h * HD, HD), HD) for h in range(per)]
        kinds = ([0] if with_ref else []) + ([1] if with_self else [])
        tasks = [(h, kind) for h in range(per) for kind in kinds]

        def scores_of(task):
            h, kind = task
            if kind == 0 or not with_ref:
                queries[h] = joined(qbuf, (b,), spans[h])
            if kind == 0:
                return dot_t(queries[h], rkey[:, spans[h]]) + bias
            return dot_t(queries[h], kself[:, spans[h]])

        queries = {}
        pending = [scores_of(task) for task in tasks[:2]]
        for place, (h, kind) in enumerate(tasks):
            if place + 2 < len(tasks):
                pending.append(scores_of(tasks[place + 2]))
            scores = pending[place]
            top = jnp.max(scores, axis=1, keepdims=True)
            weights = jnp.exp2((scores - top) * FACTOR).astype(BF16)
            value_rows = (rval, vself)[kind][:, spans[h]]
            ones = jnp.ones(value_rows.shape, BF16)
            summed = jnp.dot(
                weights, jnp.concatenate([value_rows, ones], axis=1), preferred_element_type=F32
            )
            (oref, oself)[kind][b, :, spans[h]] = summed[:, :HD]
            here = lane == ch * per + h + kind * heads
            tops = jnp.where(here, top, tops)
            totals = jnp.where(here, summed[:, HD:], totals)
        mstat[b, pl.ds(0, block), :] = tops
        lstat[b, pl.ds(0, block), :] = totals

    def lse_copy(b, offset):
        to = (z + offset) % n
        return pltpu.make_async_remote_copy(
            src_ref=lse.at[z, b],
            dst_ref=lse.at[z, b],
            send_sem=s_send.at[offset, b],
            recv_sem=s_recv.at[z, b],
            device_id={"seq": to},
            device_id_type=MESH,
        )

    def finish(b):
        tops = mstat[b, pl.ds(0, block), :] * FACTOR
        mstat[b, pl.ds(0, block), :] = tops
        lstat[b, pl.ds(0, block), :] = tops + jnp.log2(lstat[b, pl.ds(0, block), :])
        for start in range(0, padded, HD):
            turned = lstat[b, pl.ds(start, HD), :].T
            lse[z, b, :, pl.ds(start, HD)] = turned[:lanes_used, :]
        for offset in range(1, n):
            lse_copy(b, offset).start()

    gain = jnp.where(c == 0, guide_ref[0], 1.0 - guide_ref[0])
    half_lane = lax.broadcasted_iota(jnp.int32, (half, HD), 1)

    def slab_copy(index):
        return pltpu.make_async_remote_copy(
            src_ref=slab.at[index],
            dst_ref=landed.at[me],
            send_sem=v_send.at[index],
            recv_sem=v_recv.at[me],
            device_id=coords(index),
            device_id_type=MESH,
        )

    def project(b):
        for offset in range(1, n):
            source = (z + offset) % n
            pltpu.make_async_remote_copy(
                src_ref=lse.at[source, b],
                dst_ref=lse.at[source, b],
                send_sem=s_send.at[offset, b],
                recv_sem=s_recv.at[source, b],
                device_id={"seq": source},
                device_id_type=MESH,
            ).wait_recv()
        for start in range(0, padded, HD):
            span = pl.ds(start, HD)
            parts = [lse[source, b, :, span] for source in range(n)]
            top = functools.reduce(jnp.maximum, parts)
            total = sum(jnp.exp2(part - top) for part in parts)
            whole = top + jnp.log2(total)
            pad = jnp.zeros((HD - lanes_used, HD), F32)
            lstat[b, span, :] = jnp.concatenate([whole, pad], axis=0).T
        share = jnp.exp2(mstat[b, pl.ds(0, block), :] - lstat[b, pl.ds(0, block), :])
        for h in range(heads):
            span = pl.ds(h * HD, HD)
            mixed = (
                share[:, h : h + 1] * oref[b, :, span]
                + share[:, heads + h : heads + h + 1] * oself[b, :, span]
            )
            att[:, span] = mixed.astype(BF16)
        vtmp[...] = gain * dot_t(att[...], wdup[...])
        for other in range(nx):
            for branch in range(nc):
                first = other * rows + branch * 2 * half
                even = vtmp[pl.ds(first, half, stride=2), :]
                odd = vtmp[pl.ds(first + 1, half, stride=2), :]
                value = jnp.where(half_lane < outs, even, odd)
                index = (b * nx + other) * nc + branch
                slab[index, pl.ds(0, half), :] = value

                @pl.when(index != me)
                def _():
                    slab_copy(index).start()

                @pl.when(index == me)
                def _():
                    landed[index, pl.ds(0, half), :] = value

    def block_of(i):
        return z + ((i + 1) // 2) * (1 - 2 * (i % 2))

    def each_block(low, high, work):
        def one(i, carry):
            b = block_of(i)

            @pl.when((b >= 0) & (b < n))
            def _():
                work(b)

            return carry

        lax.fori_loop(low, high, one, 0)

    def clear(b, carry):
        mstat[b] = jnp.zeros((padded, HD), F32)
        lstat[b] = jnp.ones((padded, HD), F32)
        return carry

    lax.fori_loop(0, n, clear, 0)

    def own_chunk(ch, carry):
        attend(z, ch, True, False)
        return carry

    lax.fori_loop(0, chunks, own_chunk, 0)

    def step(s, carry):
        if n > 2:

            @pl.when(s == n - 1)
            def _():
                def middle(b, inner):
                    project(b)
                    return inner

                lax.fori_loop(1, n - 1, middle, 0)

        @pl.when(s == late)
        def _():
            loads[3].wait()
            loads[4].wait()
            for offset in range(1, nx):
                for kind in range(2):
                    other = (x + offset) % nx
                    target = (kbuf, vbuf)[kind].at[other]
                    pltpu.make_async_remote_copy(
                        src_ref=target,
                        dst_ref=target,
                        send_sem=kv_send.at[kind, offset],
                        recv_sem=kv_recv.at[kind, other],
                        device_id={"blk": other},
                        device_id_type=MESH,
                    ).wait_recv()
            for h in range(heads):
                span = pl.ds(h * HD, HD)
                kself[:, span] = joined(kbuf, (), span)
                vself[:, span] = joined(vbuf, (), span)

        def each_chunk(ch, inner):
            for side in range(2):
                b = z - s if side == 0 else z + s

                @pl.when((b >= 0) if side == 0 else (b < n))
                def _():
                    for offset in range(nx):
                        piece = (x + offset) % nx
                        arrived_q(b, piece, ch)
                        forward(side, b, piece, ch)

            @pl.when(s < late)
            def _():
                each_block(2 * s - 1, 2 * s + 1, lambda b: attend(b, ch, True, False))

            @pl.when(s >= late)
            def _():
                each_block(2 * s - 1, 2 * s + 1, lambda b: attend(b, ch, True, True))

            @pl.when(s == late)
            def _():
                each_block(0, 2 * late - 1, lambda b: attend(b, ch, False, True))

            return inner

        lax.fori_loop(0, chunks, each_chunk, 0)

        @pl.when(s >= late)
        def _():
            each_block(jnp.where(s == late, 0, 2 * s - 1), 2 * s + 1, finish)

        return carry

    lax.fori_loop(1, n, step, 0)

    def ends(i, carry):
        project(i * (n - 1))
        return carry

    lax.fori_loop(0, 2, ends, 0)

    for offset in range(1, nx):
        for ch in range(chunks):
            xq_copy(offset, ch).wait_send()
        for kind in range(2):
            xkv_copy(offset, kind).wait_send()

    def sent(b, carry):
        for piece in range(nx):
            for ch in range(chunks):

                @pl.when((z < n - 1) & (b <= z))
                def _():
                    z_copy(0, b, piece, ch).wait_send()

                @pl.when((z > 0) & (b >= z))
                def _():
                    z_copy(1, b, piece, ch).wait_send()

        for offset in range(1, n):
            lse_copy(b, offset).wait_send()
        return carry

    lax.fori_loop(0, n, sent, 0)

    def collect(offset, carry):
        source = (me + offset) % members
        pltpu.make_async_remote_copy(
            src_ref=slab.at[source],
            dst_ref=landed.at[source],
            send_sem=v_send.at[source],
            recv_sem=v_recv.at[source],
            device_id=coords(source),
            device_id_type=MESH,
        ).wait()
        return carry

    lax.fori_loop(1, members, collect, 0)

    guided = jnp.sum(landed[:, pl.ds(0, half), :], axis=0)
    now = jnp.full((half, HD), step_ref[0], jnp.int32)
    sig_now = sigma_of(now.astype(F32))
    sig_next = sigma_of((now + 1).astype(F32))
    delta_ref[0] = (sig_next - sig_now) * guided
    delta_ref[1] = sig_now * guided


def on_device(
    n,
    nx,
    nc,
    queries,
    keys,
    values,
    ref_keys,
    ref_values,
    ref_len,
    step_index,
    guide,
    latent,
    w_out,
):
    rows, wide = queries.shape[1:]
    refs = ref_keys.shape[1]
    width = wide // nx
    heads = width // HD
    block = nx * rows
    padded = round_up(block, HD)
    lanes_used = round_up(2 * heads, 8)
    members = n * nx * nc
    half = latent.shape[0]
    chunks = 4 if heads % 4 == 0 and heads > 4 else 1
    smem = pl.BlockSpec(memory_space=pltpu.SMEM)
    vmem = pl.BlockSpec(memory_space=pltpu.VMEM)
    anywhere = pl.BlockSpec(memory_space=pl.ANY)
    dma = pltpu.SemaphoreType.DMA
    flops = 4 * n * block * heads * HD * (refs + block)
    delta = pl.pallas_call(
        functools.partial(step_kernel, n, nx, nc, chunks),
        out_shape=jax.ShapeDtypeStruct((2,) + latent.shape, F32),
        in_specs=[smem] * 3 + [anywhere] * 6,
        out_specs=vmem,
        scratch_shapes=[
            pltpu.VMEM((n, nx, rows, width), BF16),
            pltpu.VMEM((nx, rows, width), BF16),
            pltpu.VMEM((nx, rows, width), BF16),
            pltpu.VMEM((refs, width), BF16),
            pltpu.VMEM((refs, width), BF16),
            pltpu.VMEM((2 * w_out.shape[1], width), BF16),
            pltpu.VMEM((block, width), BF16),
            pltpu.VMEM((block, width), BF16),
            pltpu.VMEM((n, block, width), F32),
            pltpu.VMEM((n, block, width), F32),
            pltpu.VMEM((n, padded, HD), F32),
            pltpu.VMEM((n, padded, HD), F32),
            pltpu.VMEM((n, n, lanes_used, padded), F32),
            pltpu.VMEM((block, width), BF16),
            pltpu.VMEM((block, HD), F32),
            pltpu.VMEM((members, round_up(half, 8), HD), F32),
            pltpu.VMEM((members, round_up(half, 8), HD), F32),
            dma((7,)),
            dma((nx, chunks)),
            dma((2, nx)),
            dma((n, nx, chunks)),
            dma((2, nx)),
            dma((2, n, nx, chunks)),
            dma((n, n)),
            dma((n, n)),
            dma((members,)),
            dma((members,)),
        ],
        compiler_params=pltpu.CompilerParams(
            collective_id=0, has_side_effects=True, vmem_limit_bytes=58 * 2**20
        ),
        cost_estimate=pl.CostEstimate(
            flops=flops, bytes_accessed=4 * refs * width * 2, transcendentals=0
        ),
    )(ref_len, step_index, guide, queries, keys, values, ref_keys, ref_values, w_out.T)
    return latent + delta[0], latent - delta[1]


def solution(mesh):
    in_specs = (
        P(("groups", "cfg"), ("seq", "blk"), None),
        P(("groups", "cfg"), ("seq", "blk"), None),
        P(("groups", "cfg"), ("seq", "blk"), None),
        P(("groups", "cfg"), "seq", None),
        P(("groups", "cfg"), "seq", None),
        P(("groups", "cfg")),
        P("groups"),
        P("groups"),
        P(("groups", "seq", "blk", "cfg"), None),
        P(),
    )
    out_specs = (P(("groups", "seq", "blk", "cfg"), None), P(("groups", "seq", "blk", "cfg"), None))
    body = functools.partial(on_device, mesh.shape["seq"], mesh.shape["blk"], mesh.shape["cfg"])
    return jax.shard_map(
        body, mesh=mesh, in_specs=in_specs, out_specs=out_specs, check_vma=False
    )
```

```python
import functools
import math

import jax
import jax.numpy as jnp
from jax import lax
from jax.experimental import pallas as pl
from jax.experimental.pallas import tpu as pltpu
from jax.sharding import PartitionSpec as P

HD = 128
STEPS = 50
FACTOR = HD ** (-0.5) * math.log2(math.e)
MESH = pl.DeviceIdType.MESH
BF16 = jnp.bfloat16
ONES = 16
F32 = jnp.float32


def round_up(value, unit):
    return (value + unit - 1) // unit * unit


def sigma_of(frac_index):
    frac = 1.0 - frac_index / STEPS
    return 5.0 * frac / (1.0 + 4.0 * frac)


def dot_t(a, b):
    return lax.dot_general(a, b, (((1,), (1,)), ((), ())), preferred_element_type=F32)


def step_kernel(
    n,
    nx,
    nc,
    chunks,
    len_ref,
    step_ref,
    guide_ref,
    q_ref,
    k_ref,
    v_ref,
    rk_ref,
    rv_ref,
    w_ref,
    delta_ref,
    qbuf,
    kbuf,
    vbuf,
    rkey,
    rval,
    wdup,
    kself,
    mask,
    rturn,
    sturn,
    oref,
    oself,
    mstat,
    lstat,
    lse,
    att,
    vwide,
    vtmp,
    slab,
    landed,
    local_sem,
    x_send,
    kv_send,
    q_recv,
    kv_recv,
    z_send,
    s_send,
    s_recv,
    v_send,
    v_recv,
):
    z = lax.axis_index("seq")
    x = lax.axis_index("blk")
    c = lax.axis_index("cfg")
    rows = q_ref.shape[1]
    width = qbuf.shape[3]
    heads = width // HD
    per = heads // chunks
    part = per * HD
    block = nx * rows
    padded = vtmp.shape[0]
    half = delta_ref.shape[1]
    refs = rkey.shape[0]
    outs = w_ref.shape[0]
    late = min(2, max(1, n - 2))

    def cols(index):
        return pl.ds(pl.multiple_of(index * width, HD), width)

    def chunk(ch):
        return pl.ds(pl.multiple_of(ch * part, HD), part)

    loads = [
        pltpu.make_async_copy(q_ref.at[0, :, cols(x)], qbuf.at[z, x], local_sem.at[0]),
        pltpu.make_async_copy(rk_ref.at[0, :, cols(x)], rkey, local_sem.at[1]),
        pltpu.make_async_copy(rv_ref.at[0, :, cols(x)], rval, local_sem.at[2]),
        pltpu.make_async_copy(k_ref.at[0, :, cols(x)], kbuf.at[x], local_sem.at[3]),
        pltpu.make_async_copy(v_ref.at[0, :, cols(x)], vbuf.at[x], local_sem.at[4]),
        pltpu.make_async_copy(w_ref.at[:, cols(x)], wdup.at[pl.ds(0, outs)], local_sem.at[5]),
        pltpu.make_async_copy(w_ref.at[:, cols(x)], wdup.at[pl.ds(outs, outs)], local_sem.at[6]),
    ]
    for load in loads:
        load.start()

    members = n * nx * nc
    me = (z * nx + x) * nc + c

    def coords(index):
        return {"seq": index // (nx * nc), "blk": (index // nc) % nx, "cfg": index % nc}

    barrier = pltpu.get_barrier_semaphore()

    def greet(offset, carry):
        pl.semaphore_signal(
            barrier, inc=1, device_id=coords((me + offset) % members), device_id_type=MESH
        )
        return carry

    lax.fori_loop(1, members, greet, 0)
    ref_index = lax.broadcasted_iota(jnp.int32, (refs, block), 0) + z * refs
    mask[...] = jnp.where(ref_index < len_ref[0], jnp.float32(0.0), jnp.float32(-1e30))
    rturn[:, pl.ds(HD, ONES), :] = jnp.ones((heads, ONES, refs), BF16)
    sturn[:, pl.ds(HD, ONES), :] = jnp.ones((heads, ONES, block), BF16)
    pl.semaphore_wait(barrier, members - 1)

    def xq_copy(offset, ch):
        to = (x + offset) % nx
        span = pl.ds(pl.multiple_of(to * width + ch * part, HD), part)
        return pltpu.make_async_remote_copy(
            src_ref=q_ref.at[0, :, span],
            dst_ref=qbuf.at[z, x, :, chunk(ch)],
            send_sem=x_send.at[offset, ch],
            recv_sem=q_recv.at[z, x, ch],
            device_id={"blk": to},
            device_id_type=MESH,
        )

    def xkv_copy(offset, kind):
        to = (x + offset) % nx
        return pltpu.make_async_remote_copy(
            src_ref=(k_ref, v_ref)[kind].at[0, :, cols(to)],
            dst_ref=(kbuf, vbuf)[kind].at[x],
            send_sem=kv_send.at[kind, offset],
            recv_sem=kv_recv.at[kind, x],
            device_id={"blk": to},
            device_id_type=MESH,
        )

    def z_copy(side, b, piece, ch):
        ref = qbuf.at[b, piece, :, chunk(ch)]
        return pltpu.make_async_remote_copy(
            src_ref=ref,
            dst_ref=ref,
            send_sem=z_send.at[side, b, piece, ch],
            recv_sem=q_recv.at[b, piece, ch],
            device_id={"seq": z + 1 - 2 * side},
            device_id_type=MESH,
        )

    def forward(side, b, piece, ch):
        @pl.when((z < n - 1) if side == 0 else (z > 0))
        def _():
            z_copy(side, b, piece, ch).start()

    def arrived_q(b, piece, ch):
        ref = qbuf.at[b, piece, :, chunk(ch)]
        pltpu.make_async_remote_copy(
            src_ref=ref,
            dst_ref=ref,
            send_sem=z_send.at[0, b, piece, ch],
            recv_sem=q_recv.at[b, piece, ch],
            device_id={"blk": (x + 1) % nx},
            device_id_type=MESH,
        ).wait_recv()

    for ch in range(chunks):
        for offset in range(1, nx):
            xq_copy(offset, ch).start()
    loads[0].wait()
    for ch in range(chunks):
        forward(0, z, x, ch)
        forward(1, z, x, ch)
    for load in loads[1:3] + loads[5:]:
        load.wait()
    for h in range(heads):
        rturn[h, pl.ds(0, HD), :] = rval[:, pl.ds(h * HD, HD)].astype(F32).T.astype(BF16)
    for ch in range(chunks):
        for offset in range(1, nx):
            piece = (x + offset) % nx
            arrived_q(z, piece, ch)
            forward(0, z, piece, ch)
            forward(1, z, piece, ch)
    for kind in range(2):
        for offset in range(1, nx):
            xkv_copy(offset, kind).start()

    def joined(ref, index, span):
        parts = [ref[index + (p, slice(None), span)].astype(F32) for p in range(nx)]
        return jnp.concatenate(parts, axis=0) if nx > 1 else parts[0]

    def attend(b, ch, with_ref, with_self):
        spans = [pl.ds(pl.multiple_of(ch * part + h * HD, HD), HD) for h in range(per)]
        kinds = ([0] if with_ref else []) + ([1] if with_self else [])
        group = min(2, per)

        def scores_of(first):
            found = []
            for h in range(first, first + group):
                query = joined(qbuf, (b,), spans[h]).astype(BF16)
                for kind in kinds:
                    scores = dot_t((rkey, kself)[kind][:, spans[h]], query)
                    found.append((h, kind, scores + mask[...] if kind == 0 else scores))
            return found

        upcoming = scores_of(0)
        for first in range(0, per, group):
            current = upcoming
            if first + group < per:
                upcoming = scores_of(first + group)
            tops = [jnp.max(scores, axis=0, keepdims=True) for _, _, scores in current]
            weights = [
                jnp.exp2((scores - top) * FACTOR).astype(BF16)
                for (_, _, scores), top in zip(current, tops)
            ]
            sums = [
                jnp.dot(
                    (rturn, sturn)[kind][ch * per + h], weight, preferred_element_type=F32
                )
                for (h, kind, _), weight in zip(current, weights)
            ]
            for (h, kind, _), top, summed in zip(current, tops, sums):
                (oref, oself)[kind][b, ch * per + h] = summed[:HD]
                row = pl.ds(ch * per + h + kind * heads, 1)
                mstat[b, row, :] = top
                lstat[b, row, :] = summed[HD : HD + 1]

    def lse_copy(b, offset):
        to = (z + offset) % n
        return pltpu.make_async_remote_copy(
            src_ref=lse.at[z, b],
            dst_ref=lse.at[z, b],
            send_sem=s_send.at[offset, b],
            recv_sem=s_recv.at[z, b],
            device_id={"seq": to},
            device_id_type=MESH,
        )

    def finish(b):
        lse[z, b] = mstat[b] * FACTOR + jnp.log2(lstat[b])
        for offset in range(1, n):
            lse_copy(b, offset).start()

    gain = jnp.where(c == 0, guide_ref[0], 1.0 - guide_ref[0])
    half_lane = lax.broadcasted_iota(jnp.int32, (half, HD), 1)

    def slab_copy(index):
        return pltpu.make_async_remote_copy(
            src_ref=slab.at[index],
            dst_ref=landed.at[me],
            send_sem=v_send.at[index],
            recv_sem=v_recv.at[me],
            device_id=coords(index),
            device_id_type=MESH,
        )

    def project(b):
        for offset in range(1, n):
            source = (z + offset) % n
            pltpu.make_async_remote_copy(
                src_ref=lse.at[source, b],
                dst_ref=lse.at[source, b],
                send_sem=s_send.at[offset, b],
                recv_sem=s_recv.at[source, b],
                device_id={"seq": source},
                device_id_type=MESH,
            ).wait_recv()
        parts = [lse[source, b] for source in range(n)]
        top = functools.reduce(jnp.maximum, parts)
        total = sum(jnp.exp2(part - top) for part in parts)
        share = jnp.exp2(mstat[b] * FACTOR - top - jnp.log2(total))
        for h in range(heads):
            mixed = (
                share[h : h + 1] * oref[b, h] + share[heads + h : heads + h + 1] * oself[b, h]
            )
            att[pl.ds(h * HD, HD), :] = mixed.astype(BF16)
        vwide[:, pl.ds(0, block)] = gain * jnp.dot(
            wdup[...], att[...], preferred_element_type=F32
        )
        for start in range(0, padded, HD):
            span = pl.ds(start, HD)
            vtmp[span, :] = vwide[:, span].T
        for other in range(nx):
            for branch in range(nc):
                first = other * rows + branch * 2 * half
                even = vtmp[pl.ds(first, half, stride=2), :]
                odd = vtmp[pl.ds(first + 1, half, stride=2), :]
                value = jnp.where(half_lane < outs, even, odd)
                index = (b * nx + other) * nc + branch
                slab[index, pl.ds(0, half), :] = value

                @pl.when(index != me)
                def _():
                    slab_copy(index).start()

                @pl.when(index == me)
                def _():
                    landed[index, pl.ds(0, half), :] = value

    def block_of(i):
        return z + ((i + 1) // 2) * (1 - 2 * (i % 2))

    def each_block(low, high, work):
        def one(i, carry):
            b = block_of(i)

            @pl.when((b >= 0) & (b < n))
            def _():
                work(b)

            return carry

        lax.fori_loop(low, high, one, 0)

    def own_chunk(ch, carry):
        attend(z, ch, True, False)
        return carry

    lax.fori_loop(0, chunks, own_chunk, 0)

    def step(s, carry):
        if n > 2:

            @pl.when(s == n - 1)
            def _():
                def middle(b, inner):
                    project(b)
                    return inner

                lax.fori_loop(1, n - 1, middle, 0)

        @pl.when(s == late)
        def _():
            loads[3].wait()
            loads[4].wait()
            for offset in range(1, nx):
                for kind in range(2):
                    other = (x + offset) % nx
                    target = (kbuf, vbuf)[kind].at[other]
                    pltpu.make_async_remote_copy(
                        src_ref=target,
                        dst_ref=target,
                        send_sem=kv_send.at[kind, offset],
                        recv_sem=kv_recv.at[kind, other],
                        device_id={"blk": other},
                        device_id_type=MESH,
                    ).wait_recv()
            for h in range(heads):
                span = pl.ds(h * HD, HD)
                kself[:, span] = joined(kbuf, (), span).astype(BF16)
                sturn[h, pl.ds(0, HD), :] = joined(vbuf, (), span).T.astype(BF16)

        def each_chunk(ch, inner):
            for side in range(2):
                b = z - s if side == 0 else z + s

                @pl.when((b >= 0) if side == 0 else (b < n))
                def _():
                    for offset in range(nx):
                        piece = (x + offset) % nx
                        arrived_q(b, piece, ch)
                        forward(side, b, piece, ch)

            @pl.when(s < late)
            def _():
                each_block(2 * s - 1, 2 * s + 1, lambda b: attend(b, ch, True, False))

            @pl.when(s >= late)
            def _():
                each_block(2 * s - 1, 2 * s + 1, lambda b: attend(b, ch, True, True))

            @pl.when(s == late)
            def _():
                each_block(0, 2 * late - 1, lambda b: attend(b, ch, False, True))

            return inner

        lax.fori_loop(0, chunks, each_chunk, 0)

        @pl.when(s >= late)
        def _():
            each_block(jnp.where(s == late, 0, 2 * s - 1), 2 * s + 1, finish)

        return carry

    lax.fori_loop(1, n, step, 0)

    def ends(i, carry):
        project(i * (n - 1))
        return carry

    lax.fori_loop(0, 2, ends, 0)

    for offset in range(1, nx):
        for ch in range(chunks):
            xq_copy(offset, ch).wait_send()
        for kind in range(2):
            xkv_copy(offset, kind).wait_send()

    def sent(b, carry):
        for piece in range(nx):
            for ch in range(chunks):

                @pl.when((z < n - 1) & (b <= z))
                def _():
                    z_copy(0, b, piece, ch).wait_send()

                @pl.when((z > 0) & (b >= z))
                def _():
                    z_copy(1, b, piece, ch).wait_send()

        for offset in range(1, n):
            lse_copy(b, offset).wait_send()
        return carry

    lax.fori_loop(0, n, sent, 0)

    def collect(offset, carry):
        source = (me + offset) % members
        pltpu.make_async_remote_copy(
            src_ref=slab.at[source],
            dst_ref=landed.at[source],
            send_sem=v_send.at[source],
            recv_sem=v_recv.at[source],
            device_id=coords(source),
            device_id_type=MESH,
        ).wait()
        return carry

    lax.fori_loop(1, members, collect, 0)

    guided = jnp.sum(landed[:, pl.ds(0, half), :], axis=0)
    now = jnp.full((half, HD), step_ref[0], jnp.int32)
    sig_now = sigma_of(now.astype(F32))
    sig_next = sigma_of((now + 1).astype(F32))
    delta_ref[0] = (sig_next - sig_now) * guided
    delta_ref[1] = sig_now * guided


def on_device(
    n,
    nx,
    nc,
    queries,
    keys,
    values,
    ref_keys,
    ref_values,
    ref_len,
    step_index,
    guide,
    latent,
    w_out,
):
    rows, wide = queries.shape[1:]
    refs = ref_keys.shape[1]
    width = wide // nx
    heads = width // HD
    block = nx * rows
    padded = round_up(block, HD)
    stats = round_up(2 * heads, 8)
    members = n * nx * nc
    half = latent.shape[0]
    chunks = 4 if heads % 4 == 0 and heads > 4 else 1
    smem = pl.BlockSpec(memory_space=pltpu.SMEM)
    vmem = pl.BlockSpec(memory_space=pltpu.VMEM)
    anywhere = pl.BlockSpec(memory_space=pl.ANY)
    dma = pltpu.SemaphoreType.DMA
    flops = 4 * n * block * heads * HD * (refs + block)
    delta = pl.pallas_call(
        functools.partial(step_kernel, n, nx, nc, chunks),
        out_shape=jax.ShapeDtypeStruct((2,) + latent.shape, F32),
        in_specs=[smem] * 3 + [anywhere] * 6,
        out_specs=vmem,
        scratch_shapes=[
            pltpu.VMEM((n, nx, rows, width), BF16),
            pltpu.VMEM((nx, rows, width), BF16),
            pltpu.VMEM((nx, rows, width), BF16),
            pltpu.VMEM((refs, width), BF16),
            pltpu.VMEM((refs, width), BF16),
            pltpu.VMEM((2 * w_out.shape[1], width), BF16),
            pltpu.VMEM((block, width), BF16),
            pltpu.VMEM((refs, block), F32),
            pltpu.VMEM((heads, HD + ONES, refs), BF16),
            pltpu.VMEM((heads, HD + ONES, block), BF16),
            pltpu.VMEM((n, heads, HD, block), F32),
            pltpu.VMEM((n, heads, HD, block), F32),
            pltpu.VMEM((n, stats, block), F32),
            pltpu.VMEM((n, stats, block), F32),
            pltpu.VMEM((n, n, stats, block), F32),
            pltpu.VMEM((width, block), BF16),
            pltpu.VMEM((HD, padded), F32),
            pltpu.VMEM((padded, HD), F32),
            pltpu.VMEM((members, round_up(half, 8), HD), F32),
            pltpu.VMEM((members, round_up(half, 8), HD), F32),
            dma((7,)),
            dma((nx, chunks)),
            dma((2, nx)),
            dma((n, nx, chunks)),
            dma((2, nx)),
            dma((2, n, nx, chunks)),
            dma((n, n)),
            dma((n, n)),
            dma((members,)),
            dma((members,)),
        ],
        compiler_params=pltpu.CompilerParams(
            collective_id=0, has_side_effects=True, vmem_limit_bytes=58 * 2**20
        ),
        cost_estimate=pl.CostEstimate(
            flops=flops, bytes_accessed=4 * refs * width * 2, transcendentals=0
        ),
    )(ref_len, step_index, guide, queries, keys, values, ref_keys, ref_values, w_out.T)
    return latent + delta[0], latent - delta[1]


def solution(mesh):
    in_specs = (
        P(("groups", "cfg"), ("seq", "blk"), None),
        P(("groups", "cfg"), ("seq", "blk"), None),
        P(("groups", "cfg"), ("seq", "blk"), None),
        P(("groups", "cfg"), "seq", None),
        P(("groups", "cfg"), "seq", None),
        P(("groups", "cfg")),
        P("groups"),
        P("groups"),
        P(("groups", "seq", "blk", "cfg"), None),
        P(),
    )
    out_specs = (P(("groups", "seq", "blk", "cfg"), None), P(("groups", "seq", "blk", "cfg"), None))
    body = functools.partial(on_device, mesh.shape["seq"], mesh.shape["blk"], mesh.shape["cfg"])
    return jax.shard_map(
        body, mesh=mesh, in_specs=in_specs, out_specs=out_specs, check_vma=False
    )
```

```python
import functools
import math

import jax
import jax.numpy as jnp
from jax import lax
from jax.experimental import pallas as pl
from jax.experimental.pallas import tpu as pltpu
from jax.sharding import PartitionSpec as P

HD = 128
STEPS = 50
FACTOR = HD ** (-0.5) * math.log2(math.e)
MESH = pl.DeviceIdType.MESH
BF16 = jnp.bfloat16
ONES = 16
F32 = jnp.float32


def round_up(value, unit):
    return (value + unit - 1) // unit * unit


def sigma_of(frac_index):
    frac = 1.0 - frac_index / STEPS
    return 5.0 * frac / (1.0 + 4.0 * frac)


def dot_t(a, b):
    return lax.dot_general(a, b, (((1,), (1,)), ((), ())), preferred_element_type=F32)


def step_kernel(
    n,
    nx,
    nc,
    chunks,
    len_ref,
    step_ref,
    guide_ref,
    q_ref,
    k_ref,
    v_ref,
    rk_ref,
    rv_ref,
    w_ref,
    delta_ref,
    qbuf,
    kbuf,
    vbuf,
    rkey,
    rval,
    wdup,
    kself,
    mask,
    rturn,
    sturn,
    oref,
    oself,
    mstat,
    lstat,
    lse,
    att,
    vwide,
    vtmp,
    slab,
    landed,
    local_sem,
    x_send,
    kv_send,
    q_recv,
    kv_recv,
    z_send,
    s_send,
    s_recv,
    v_send,
    v_recv,
):
    z = lax.axis_index("seq")
    x = lax.axis_index("blk")
    c = lax.axis_index("cfg")
    rows = q_ref.shape[1]
    width = qbuf.shape[3]
    heads = width // HD
    per = heads // chunks
    part = per * HD
    block = nx * rows
    padded = vtmp.shape[0]
    half = delta_ref.shape[1]
    refs = rkey.shape[0]
    outs = w_ref.shape[0]
    late = min(2, n - 1)

    def cols(index):
        return pl.ds(pl.multiple_of(index * width, HD), width)

    def chunk(ch):
        return pl.ds(pl.multiple_of(ch * part, HD), part)

    loads = [
        pltpu.make_async_copy(q_ref.at[0, :, cols(x)], qbuf.at[z, x], local_sem.at[0]),
        pltpu.make_async_copy(rk_ref.at[0, :, cols(x)], rkey, local_sem.at[1]),
        pltpu.make_async_copy(rv_ref.at[0, :, cols(x)], rval, local_sem.at[2]),
        pltpu.make_async_copy(k_ref.at[0, :, cols(x)], kbuf.at[x], local_sem.at[3]),
        pltpu.make_async_copy(v_ref.at[0, :, cols(x)], vbuf.at[x], local_sem.at[4]),
        pltpu.make_async_copy(w_ref.at[:, cols(x)], wdup.at[pl.ds(0, outs)], local_sem.at[5]),
        pltpu.make_async_copy(w_ref.at[:, cols(x)], wdup.at[pl.ds(outs, outs)], local_sem.at[6]),
    ]
    for load in loads:
        load.start()

    members = n * nx * nc
    me = (z * nx + x) * nc + c

    def coords(index):
        return {"seq": index // (nx * nc), "blk": (index // nc) % nx, "cfg": index % nc}

    barrier = pltpu.get_barrier_semaphore()

    def greet(offset, carry):
        pl.semaphore_signal(
            barrier, inc=1, device_id=coords((me + offset) % members), device_id_type=MESH
        )
        return carry

    lax.fori_loop(1, members, greet, 0)
    ref_index = lax.broadcasted_iota(jnp.int32, (refs, block), 0) + z * refs
    mask[...] = jnp.where(ref_index < len_ref[0], jnp.float32(0.0), jnp.float32(-1e30))
    rturn[:, pl.ds(HD, ONES), :] = jnp.ones((heads, ONES, refs), BF16)
    sturn[:, pl.ds(HD, ONES), :] = jnp.ones((heads, ONES, block), BF16)
    pl.semaphore_wait(barrier, members - 1)

    def xq_copy(offset, ch):
        to = (x + offset) % nx
        span = pl.ds(pl.multiple_of(to * width + ch * part, HD), part)
        return pltpu.make_async_remote_copy(
            src_ref=q_ref.at[0, :, span],
            dst_ref=qbuf.at[z, x, :, chunk(ch)],
            send_sem=x_send.at[offset, ch],
            recv_sem=q_recv.at[z, x, ch],
            device_id={"blk": to},
            device_id_type=MESH,
        )

    def xkv_copy(offset, kind):
        to = (x + offset) % nx
        return pltpu.make_async_remote_copy(
            src_ref=(k_ref, v_ref)[kind].at[0, :, cols(to)],
            dst_ref=(kbuf, vbuf)[kind].at[x],
            send_sem=kv_send.at[kind, offset],
            recv_sem=kv_recv.at[kind, x],
            device_id={"blk": to},
            device_id_type=MESH,
        )

    def z_copy(side, b, piece, ch):
        ref = qbuf.at[b, piece, :, chunk(ch)]
        return pltpu.make_async_remote_copy(
            src_ref=ref,
            dst_ref=ref,
            send_sem=z_send.at[side, b, piece, ch],
            recv_sem=q_recv.at[b, piece, ch],
            device_id={"seq": z + 1 - 2 * side},
            device_id_type=MESH,
        )

    def forward(side, b, piece, ch):
        @pl.when((z < n - 1) if side == 0 else (z > 0))
        def _():
            z_copy(side, b, piece, ch).start()

    def arrived_q(b, piece, ch):
        ref = qbuf.at[b, piece, :, chunk(ch)]
        pltpu.make_async_remote_copy(
            src_ref=ref,
            dst_ref=ref,
            send_sem=z_send.at[0, b, piece, ch],
            recv_sem=q_recv.at[b, piece, ch],
            device_id={"blk": (x + 1) % nx},
            device_id_type=MESH,
        ).wait_recv()

    for ch in range(chunks):
        for offset in range(1, nx):
            xq_copy(offset, ch).start()
    loads[0].wait()
    for ch in range(chunks):
        forward(0, z, x, ch)
        forward(1, z, x, ch)
    for ch in range(chunks):
        for offset in range(1, nx):
            piece = (x + offset) % nx
            arrived_q(z, piece, ch)
            forward(0, z, piece, ch)
            forward(1, z, piece, ch)
    for kind in range(2):
        for offset in range(1, nx):
            xkv_copy(offset, kind).start()

    def joined(ref, index, span):
        parts = [ref[index + (p, slice(None), span)].astype(F32) for p in range(nx)]
        return jnp.concatenate(parts, axis=0) if nx > 1 else parts[0]

    def attend(b, ch, with_ref, with_self):
        spans = [pl.ds(pl.multiple_of(ch * part + h * HD, HD), HD) for h in range(per)]
        kinds = ([0] if with_ref else []) + ([1] if with_self else [])
        group = min(2, per)

        def scores_of(first):
            found = []
            for h in range(first, first + group):
                query = joined(qbuf, (b,), spans[h]).astype(BF16)
                for kind in kinds:
                    scores = dot_t((rkey, kself)[kind][:, spans[h]], query)
                    found.append((h, kind, scores + mask[...] if kind == 0 else scores))
            return found

        upcoming = scores_of(0)
        for first in range(0, per, group):
            current = upcoming
            if first + group < per:
                upcoming = scores_of(first + group)
            tops = [jnp.max(scores, axis=0, keepdims=True) for _, _, scores in current]
            weights = [
                jnp.exp2((scores - top) * FACTOR).astype(BF16)
                for (_, _, scores), top in zip(current, tops)
            ]
            sums = [
                jnp.dot(
                    (rturn, sturn)[kind][ch * per + h], weight, preferred_element_type=F32
                )
                for (h, kind, _), weight in zip(current, weights)
            ]
            for (h, kind, _), top, summed in zip(current, tops, sums):
                (oref, oself)[kind][b, ch * per + h] = summed[:HD]
                row = pl.ds(ch * per + h + kind * heads, 1)
                mstat[b, row, :] = top
                lstat[b, row, :] = summed[HD : HD + 1]

    def lse_copy(b, offset):
        to = (z + offset) % n
        return pltpu.make_async_remote_copy(
            src_ref=lse.at[z, b],
            dst_ref=lse.at[z, b],
            send_sem=s_send.at[offset, b],
            recv_sem=s_recv.at[z, b],
            device_id={"seq": to},
            device_id_type=MESH,
        )

    def finish(b):
        lse[z, b] = mstat[b] * FACTOR + jnp.log2(lstat[b])
        for offset in range(1, n):
            lse_copy(b, offset).start()

    gain = jnp.where(c == 0, guide_ref[0], 1.0 - guide_ref[0])
    half_lane = lax.broadcasted_iota(jnp.int32, (half, HD), 1)

    def slab_copy(index):
        return pltpu.make_async_remote_copy(
            src_ref=slab.at[index],
            dst_ref=landed.at[me],
            send_sem=v_send.at[index],
            recv_sem=v_recv.at[me],
            device_id=coords(index),
            device_id_type=MESH,
        )

    def project(b):
        for offset in range(1, n):
            source = (z + offset) % n
            pltpu.make_async_remote_copy(
                src_ref=lse.at[source, b],
                dst_ref=lse.at[source, b],
                send_sem=s_send.at[offset, b],
                recv_sem=s_recv.at[source, b],
                device_id={"seq": source},
                device_id_type=MESH,
            ).wait_recv()
        parts = [lse[source, b] for source in range(n)]
        top = functools.reduce(jnp.maximum, parts)
        total = sum(jnp.exp2(part - top) for part in parts)
        share = jnp.exp2(mstat[b] * FACTOR - top - jnp.log2(total))
        for h in range(heads):
            mixed = (
                share[h : h + 1] * oref[b, h] + share[heads + h : heads + h + 1] * oself[b, h]
            )
            att[pl.ds(h * HD, HD), :] = mixed.astype(BF16)
        vwide[:, pl.ds(0, block)] = gain * jnp.dot(
            wdup[...], att[...], preferred_element_type=F32
        )
        for start in range(0, padded, HD):
            span = pl.ds(start, HD)
            vtmp[span, :] = vwide[:, span].T
        for other in range(nx):
            for branch in range(nc):
                first = other * rows + branch * 2 * half
                even = vtmp[pl.ds(first, half, stride=2), :]
                odd = vtmp[pl.ds(first + 1, half, stride=2), :]
                value = jnp.where(half_lane < outs, even, odd)
                index = (b * nx + other) * nc + branch
                slab[index, pl.ds(0, half), :] = value

                @pl.when(index != me)
                def _():
                    slab_copy(index).start()

                @pl.when(index == me)
                def _():
                    landed[index, pl.ds(0, half), :] = value

    def block_of(i):
        return z + ((i + 1) // 2) * (1 - 2 * (i % 2))

    def each_block(low, high, work):
        def one(i, carry):
            b = block_of(i)

            @pl.when((b >= 0) & (b < n))
            def _():
                work(b)

            return carry

        lax.fori_loop(low, high, one, 0)

    def receive(s, ch):
        for side in range(2):
            b = z - s if side == 0 else z + s

            @pl.when((b >= 0) if side == 0 else (b < n))
            def _():
                for offset in range(nx):
                    piece = (x + offset) % nx
                    arrived_q(b, piece, ch)
                    forward(side, b, piece, ch)

    def each_chunk(work):
        def one(ch, carry):
            work(ch)
            return carry

        lax.fori_loop(0, chunks, one, 0)

    for load in loads[1:3] + loads[5:]:
        load.wait()

    def own_chunk(ch):
        receive(1, ch)
        for h in range(per):
            span = pl.ds(pl.multiple_of(ch * part + h * HD, HD), HD)
            turned = rval[:, span].astype(F32).T
            rturn[ch * per + h, pl.ds(0, HD), :] = turned.astype(BF16)
        attend(z, ch, True, False)

    each_chunk(own_chunk)
    if late > 1:
        each_chunk(lambda ch: each_block(1, 3, lambda b: attend(b, ch, True, False)))

    def step(s, carry):
        @pl.when(s == late)
        def _():
            if late > 1:
                each_chunk(lambda ch: receive(s, ch))
            loads[3].wait()
            loads[4].wait()
            for offset in range(1, nx):
                for kind in range(2):
                    other = (x + offset) % nx
                    target = (kbuf, vbuf)[kind].at[other]
                    pltpu.make_async_remote_copy(
                        src_ref=target,
                        dst_ref=target,
                        send_sem=kv_send.at[kind, offset],
                        recv_sem=kv_recv.at[kind, other],
                        device_id={"blk": other},
                        device_id_type=MESH,
                    ).wait_recv()
            for h in range(heads):
                span = pl.ds(h * HD, HD)
                kself[:, span] = joined(kbuf, (), span).astype(BF16)
                sturn[h, pl.ds(0, HD), :] = joined(vbuf, (), span).T.astype(BF16)

        def work(ch):
            @pl.when(s > late)
            def _():
                receive(s, ch)

            each_block(2 * s - 1, 2 * s + 1, lambda b: attend(b, ch, True, True))

        each_chunk(work)
        each_block(2 * s - 1, 2 * s + 1, finish)

        @pl.when(s == late)
        def _():
            each_chunk(
                lambda ch: each_block(0, 2 * late - 1, lambda b: attend(b, ch, False, True))
            )
            each_block(0, 2 * late - 1, finish)

        return carry

    lax.fori_loop(late, n, step, 0)

    def middle(b, carry):
        project(b)
        return carry

    lax.fori_loop(1, n - 1, middle, 0)

    def ends(i, carry):
        project(i * (n - 1))
        return carry

    lax.fori_loop(0, 2, ends, 0)

    for offset in range(1, nx):
        for ch in range(chunks):
            xq_copy(offset, ch).wait_send()
        for kind in range(2):
            xkv_copy(offset, kind).wait_send()

    def sent(b, carry):
        for piece in range(nx):
            for ch in range(chunks):

                @pl.when((z < n - 1) & (b <= z))
                def _():
                    z_copy(0, b, piece, ch).wait_send()

                @pl.when((z > 0) & (b >= z))
                def _():
                    z_copy(1, b, piece, ch).wait_send()

        for offset in range(1, n):
            lse_copy(b, offset).wait_send()
        return carry

    lax.fori_loop(0, n, sent, 0)

    def collect(offset, carry):
        source = (me + offset) % members
        pltpu.make_async_remote_copy(
            src_ref=slab.at[source],
            dst_ref=landed.at[source],
            send_sem=v_send.at[source],
            recv_sem=v_recv.at[source],
            device_id=coords(source),
            device_id_type=MESH,
        ).wait()
        return carry

    lax.fori_loop(1, members, collect, 0)

    guided = jnp.sum(landed[:, pl.ds(0, half), :], axis=0)
    now = jnp.full((half, HD), step_ref[0], jnp.int32)
    sig_now = sigma_of(now.astype(F32))
    sig_next = sigma_of((now + 1).astype(F32))
    delta_ref[0] = (sig_next - sig_now) * guided
    delta_ref[1] = sig_now * guided


def on_device(
    n,
    nx,
    nc,
    queries,
    keys,
    values,
    ref_keys,
    ref_values,
    ref_len,
    step_index,
    guide,
    latent,
    w_out,
):
    rows, wide = queries.shape[1:]
    refs = ref_keys.shape[1]
    width = wide // nx
    heads = width // HD
    block = nx * rows
    padded = round_up(block, HD)
    stats = round_up(2 * heads, 8)
    members = n * nx * nc
    half = latent.shape[0]
    chunks = 4 if heads % 4 == 0 and heads > 4 else 1
    smem = pl.BlockSpec(memory_space=pltpu.SMEM)
    vmem = pl.BlockSpec(memory_space=pltpu.VMEM)
    anywhere = pl.BlockSpec(memory_space=pl.ANY)
    dma = pltpu.SemaphoreType.DMA
    flops = 4 * n * block * heads * HD * (refs + block)
    delta = pl.pallas_call(
        functools.partial(step_kernel, n, nx, nc, chunks),
        out_shape=jax.ShapeDtypeStruct((2,) + latent.shape, F32),
        in_specs=[smem] * 3 + [anywhere] * 6,
        out_specs=vmem,
        scratch_shapes=[
            pltpu.VMEM((n, nx, rows, width), BF16),
            pltpu.VMEM((nx, rows, width), BF16),
            pltpu.VMEM((nx, rows, width), BF16),
            pltpu.VMEM((refs, width), BF16),
            pltpu.VMEM((refs, width), BF16),
            pltpu.VMEM((2 * w_out.shape[1], width), BF16),
            pltpu.VMEM((block, width), BF16),
            pltpu.VMEM((refs, block), F32),
            pltpu.VMEM((heads, HD + ONES, refs), BF16),
            pltpu.VMEM((heads, HD + ONES, block), BF16),
            pltpu.VMEM((n, heads, HD, block), F32),
            pltpu.VMEM((n, heads, HD, block), F32),
            pltpu.VMEM((n, stats, block), F32),
            pltpu.VMEM((n, stats, block), F32),
            pltpu.VMEM((n, n, stats, block), F32),
            pltpu.VMEM((width, block), BF16),
            pltpu.VMEM((HD, padded), F32),
            pltpu.VMEM((padded, HD), F32),
            pltpu.VMEM((members, round_up(half, 8), HD), F32),
            pltpu.VMEM((members, round_up(half, 8), HD), F32),
            dma((7,)),
            dma((nx, chunks)),
            dma((2, nx)),
            dma((n, nx, chunks)),
            dma((2, nx)),
            dma((2, n, nx, chunks)),
            dma((n, n)),
            dma((n, n)),
            dma((members,)),
            dma((members,)),
        ],
        compiler_params=pltpu.CompilerParams(
            collective_id=0, has_side_effects=True, vmem_limit_bytes=58 * 2**20
        ),
        cost_estimate=pl.CostEstimate(
            flops=flops, bytes_accessed=4 * refs * width * 2, transcendentals=0
        ),
    )(ref_len, step_index, guide, queries, keys, values, ref_keys, ref_values, w_out.T)
    return latent + delta[0], latent - delta[1]


def solution(mesh):
    in_specs = (
        P(("groups", "cfg"), ("seq", "blk"), None),
        P(("groups", "cfg"), ("seq", "blk"), None),
        P(("groups", "cfg"), ("seq", "blk"), None),
        P(("groups", "cfg"), "seq", None),
        P(("groups", "cfg"), "seq", None),
        P(("groups", "cfg")),
        P("groups"),
        P("groups"),
        P(("groups", "seq", "blk", "cfg"), None),
        P(),
    )
    out_specs = (P(("groups", "seq", "blk", "cfg"), None), P(("groups", "seq", "blk", "cfg"), None))
    body = functools.partial(on_device, mesh.shape["seq"], mesh.shape["blk"], mesh.shape["cfg"])
    return jax.shard_map(
        body, mesh=mesh, in_specs=in_specs, out_specs=out_specs, check_vma=False
    )
```

```python
import functools
import math

import jax
import jax.numpy as jnp
from jax import lax
from jax.experimental import pallas as pl
from jax.experimental.pallas import tpu as pltpu
from jax.sharding import PartitionSpec as P

HD = 128
STEPS = 50
FACTOR = HD ** (-0.5) * math.log2(math.e)
MESH = pl.DeviceIdType.MESH
BF16 = jnp.bfloat16
ONES = 16
F32 = jnp.float32


def round_up(value, unit):
    return (value + unit - 1) // unit * unit


def sigma_of(frac_index):
    frac = 1.0 - frac_index / STEPS
    return 5.0 * frac / (1.0 + 4.0 * frac)


def dot_t(a, b):
    return lax.dot_general(a, b, (((1,), (1,)), ((), ())), preferred_element_type=F32)


def step_kernel(
    n,
    nx,
    nc,
    chunks,
    len_ref,
    step_ref,
    guide_ref,
    q_ref,
    k_ref,
    v_ref,
    rk_ref,
    rv_ref,
    w_ref,
    delta_ref,
    qbuf,
    kbuf,
    vbuf,
    rkey,
    rval,
    wdup,
    kself,
    mask,
    rturn,
    sturn,
    oref,
    oself,
    mstat,
    lstat,
    lse,
    att,
    vwide,
    vtmp,
    slab,
    landed,
    local_sem,
    x_send,
    kv_send,
    q_recv,
    kv_recv,
    z_send,
    s_send,
    s_recv,
    v_send,
    v_recv,
):
    z = lax.axis_index("seq")
    x = lax.axis_index("blk")
    c = lax.axis_index("cfg")
    rows = q_ref.shape[1]
    width = qbuf.shape[3]
    heads = width // HD
    per = heads // chunks
    part = per * HD
    block = nx * rows
    padded = vtmp.shape[0]
    half = delta_ref.shape[1]
    refs = rkey.shape[0]
    outs = w_ref.shape[0]
    late = min(2, n - 1)

    def cols(index):
        return pl.ds(pl.multiple_of(index * width, HD), width)

    def chunk(ch):
        return pl.ds(pl.multiple_of(ch * part, HD), part)

    loads = [
        pltpu.make_async_copy(q_ref.at[0, :, cols(x)], qbuf.at[z, x], local_sem.at[0]),
        pltpu.make_async_copy(rk_ref.at[0, :, cols(x)], rkey, local_sem.at[1]),
        pltpu.make_async_copy(rv_ref.at[0, :, cols(x)], rval, local_sem.at[2]),
        pltpu.make_async_copy(k_ref.at[0, :, cols(x)], kbuf.at[x], local_sem.at[3]),
        pltpu.make_async_copy(v_ref.at[0, :, cols(x)], vbuf.at[x], local_sem.at[4]),
        pltpu.make_async_copy(w_ref.at[:, cols(x)], wdup.at[pl.ds(0, outs)], local_sem.at[5]),
        pltpu.make_async_copy(w_ref.at[:, cols(x)], wdup.at[pl.ds(outs, outs)], local_sem.at[6]),
    ]
    for load in loads:
        load.start()

    members = n * nx * nc
    me = (z * nx + x) * nc + c

    def coords(index):
        return {"seq": index // (nx * nc), "blk": (index // nc) % nx, "cfg": index % nc}

    barrier = pltpu.get_barrier_semaphore()

    def greet(offset, carry):
        pl.semaphore_signal(
            barrier, inc=1, device_id=coords((me + offset) % members), device_id_type=MESH
        )
        return carry

    lax.fori_loop(1, members, greet, 0)
    ref_index = lax.broadcasted_iota(jnp.int32, (refs, block), 0) + z * refs
    mask[...] = jnp.where(ref_index < len_ref[0], jnp.float32(0.0), jnp.float32(-1e30))
    rturn[:, pl.ds(HD, ONES), :] = jnp.ones((heads, ONES, refs), BF16)
    sturn[:, pl.ds(HD, ONES), :] = jnp.ones((heads, ONES, block), BF16)
    pl.semaphore_wait(barrier, members - 1)

    def xq_copy(offset, ch):
        to = (x + offset) % nx
        span = pl.ds(pl.multiple_of(to * width + ch * part, HD), part)
        return pltpu.make_async_remote_copy(
            src_ref=q_ref.at[0, :, span],
            dst_ref=qbuf.at[z, x, :, chunk(ch)],
            send_sem=x_send.at[offset, ch],
            recv_sem=q_recv.at[z, x, ch],
            device_id={"blk": to},
            device_id_type=MESH,
        )

    def xkv_copy(offset, kind):
        to = (x + offset) % nx
        return pltpu.make_async_remote_copy(
            src_ref=(k_ref, v_ref)[kind].at[0, :, cols(to)],
            dst_ref=(kbuf, vbuf)[kind].at[x],
            send_sem=kv_send.at[kind, offset],
            recv_sem=kv_recv.at[kind, x],
            device_id={"blk": to},
            device_id_type=MESH,
        )

    def z_copy(side, b, piece, ch):
        ref = qbuf.at[b, piece, :, chunk(ch)]
        return pltpu.make_async_remote_copy(
            src_ref=ref,
            dst_ref=ref,
            send_sem=z_send.at[side, b, piece, ch],
            recv_sem=q_recv.at[b, piece, ch],
            device_id={"seq": z + 1 - 2 * side},
            device_id_type=MESH,
        )

    def forward(side, b, piece, ch):
        @pl.when((z < n - 1) if side == 0 else (z > 0))
        def _():
            z_copy(side, b, piece, ch).start()

    def arrived_q(b, piece, ch):
        ref = qbuf.at[b, piece, :, chunk(ch)]
        pltpu.make_async_remote_copy(
            src_ref=ref,
            dst_ref=ref,
            send_sem=z_send.at[0, b, piece, ch],
            recv_sem=q_recv.at[b, piece, ch],
            device_id={"blk": (x + 1) % nx},
            device_id_type=MESH,
        ).wait_recv()

    for ch in range(chunks):
        for offset in range(1, nx):
            xq_copy(offset, ch).start()
    loads[0].wait()
    for ch in range(chunks):
        forward(0, z, x, ch)
        forward(1, z, x, ch)
    for ch in range(chunks):
        for offset in range(1, nx):
            piece = (x + offset) % nx
            arrived_q(z, piece, ch)
            forward(0, z, piece, ch)
            forward(1, z, piece, ch)
    for kind in range(2):
        for offset in range(1, nx):
            xkv_copy(offset, kind).start()

    def joined(ref, index, span):
        parts = [ref[index + (p, slice(None), span)].astype(F32) for p in range(nx)]
        return jnp.concatenate(parts, axis=0) if nx > 1 else parts[0]

    def attend(b, ch, with_ref, with_self):
        spans = [pl.ds(pl.multiple_of(ch * part + h * HD, HD), HD) for h in range(per)]
        kinds = ([0] if with_ref else []) + ([1] if with_self else [])
        group = min(2, per)

        def scores_of(first):
            found = []
            for h in range(first, first + group):
                query = joined(qbuf, (b,), spans[h]).astype(BF16)
                for kind in kinds:
                    scores = dot_t((rkey, kself)[kind][:, spans[h]], query)
                    found.append((h, kind, scores + mask[...] if kind == 0 else scores))
            return found

        upcoming = scores_of(0)
        for first in range(0, per, group):
            current = upcoming
            if first + group < per:
                upcoming = scores_of(first + group)
            tops = [jnp.max(scores, axis=0, keepdims=True) for _, _, scores in current]
            weights = [
                jnp.exp2((scores - top) * FACTOR).astype(BF16)
                for (_, _, scores), top in zip(current, tops)
            ]
            sums = [
                jnp.dot(
                    (rturn, sturn)[kind][ch * per + h], weight, preferred_element_type=F32
                )
                for (h, kind, _), weight in zip(current, weights)
            ]
            for (h, kind, _), top, summed in zip(current, tops, sums):
                (oref, oself)[kind][b, ch * per + h] = summed[:HD]
                row = pl.ds(ch * per + h + kind * heads, 1)
                mstat[b, row, :] = top
                lstat[b, row, :] = summed[HD : HD + 1]

    def lse_copy(b, offset):
        to = (z + offset) % n
        return pltpu.make_async_remote_copy(
            src_ref=lse.at[z, b],
            dst_ref=lse.at[z, b],
            send_sem=s_send.at[offset, b],
            recv_sem=s_recv.at[z, b],
            device_id={"seq": to},
            device_id_type=MESH,
        )

    def finish(b):
        lse[z, b] = mstat[b] * FACTOR + jnp.log2(lstat[b])
        for offset in range(1, n):
            lse_copy(b, offset).start()

    gain = jnp.where(c == 0, guide_ref[0], 1.0 - guide_ref[0])
    half_lane = lax.broadcasted_iota(jnp.int32, (half, HD), 1)

    def slab_copy(index):
        return pltpu.make_async_remote_copy(
            src_ref=slab.at[index],
            dst_ref=landed.at[me],
            send_sem=v_send.at[index],
            recv_sem=v_recv.at[me],
            device_id=coords(index),
            device_id_type=MESH,
        )

    def project(b):
        for offset in range(1, n):
            source = (z + offset) % n
            pltpu.make_async_remote_copy(
                src_ref=lse.at[source, b],
                dst_ref=lse.at[source, b],
                send_sem=s_send.at[offset, b],
                recv_sem=s_recv.at[source, b],
                device_id={"seq": source},
                device_id_type=MESH,
            ).wait_recv()
        parts = [lse[source, b] for source in range(n)]
        top = functools.reduce(jnp.maximum, parts)
        total = sum(jnp.exp2(part - top) for part in parts)
        share = jnp.exp2(mstat[b] * FACTOR - top - jnp.log2(total))
        for h in range(heads):
            mixed = (
                share[h : h + 1] * oref[b, h] + share[heads + h : heads + h + 1] * oself[b, h]
            )
            att[pl.ds(h * HD, HD), :] = mixed.astype(BF16)
        vwide[:, pl.ds(0, block)] = gain * jnp.dot(
            wdup[...], att[...], preferred_element_type=F32
        )
        for start in range(0, padded, HD):
            span = pl.ds(start, HD)
            vtmp[span, :] = vwide[:, span].T
        for other in range(nx):
            for branch in range(nc):
                first = other * rows + branch * 2 * half
                even = vtmp[pl.ds(first, half, stride=2), :]
                odd = vtmp[pl.ds(first + 1, half, stride=2), :]
                value = jnp.where(half_lane < outs, even, odd)
                index = (b * nx + other) * nc + branch
                slab[index, pl.ds(0, half), :] = value

                @pl.when(index != me)
                def _():
                    slab_copy(index).start()

                @pl.when(index == me)
                def _():
                    landed[index, pl.ds(0, half), :] = value

    def block_of(i):
        return z + ((i + 1) // 2) * (1 - 2 * (i % 2))

    def each_block(low, high, work):
        def one(i, carry):
            b = block_of(i)

            @pl.when((b >= 0) & (b < n))
            def _():
                work(b)

            return carry

        lax.fori_loop(low, high, one, 0)

    def receive(s, ch):
        for side in range(2):
            b = z - s if side == 0 else z + s

            @pl.when((b >= 0) if side == 0 else (b < n))
            def _():
                for offset in range(nx):
                    piece = (x + offset) % nx
                    arrived_q(b, piece, ch)
                    forward(side, b, piece, ch)

    def each_chunk(work):
        def one(ch, carry):
            work(ch)
            return carry

        lax.fori_loop(0, chunks, one, 0)

    for load in loads[1:3] + loads[5:]:
        load.wait()

    def own_chunk(ch):
        receive(1, ch)
        for h in range(per):
            span = pl.ds(pl.multiple_of(ch * part + h * HD, HD), HD)
            turned = rval[:, span].astype(F32).T
            rturn[ch * per + h, pl.ds(0, HD), :] = turned.astype(BF16)
        attend(z, ch, True, False)

    each_chunk(own_chunk)
    if late > 1:

        def next_chunk(ch):
            each_block(1, 3, lambda b: attend(b, ch, True, False))
            receive(2, ch)

        each_chunk(next_chunk)

    def step(s, carry):
        @pl.when(s == late)
        def _():
            loads[3].wait()
            loads[4].wait()
            for offset in range(1, nx):
                for kind in range(2):
                    other = (x + offset) % nx
                    target = (kbuf, vbuf)[kind].at[other]
                    pltpu.make_async_remote_copy(
                        src_ref=target,
                        dst_ref=target,
                        send_sem=kv_send.at[kind, offset],
                        recv_sem=kv_recv.at[kind, other],
                        device_id={"blk": other},
                        device_id_type=MESH,
                    ).wait_recv()
            for h in range(heads):
                span = pl.ds(h * HD, HD)
                kself[:, span] = joined(kbuf, (), span).astype(BF16)
                sturn[h, pl.ds(0, HD), :] = joined(vbuf, (), span).T.astype(BF16)

        def work(ch):
            @pl.when(s > late)
            def _():
                receive(s, ch)

            each_block(2 * s - 1, 2 * s + 1, lambda b: attend(b, ch, True, True))

        each_chunk(work)
        each_block(2 * s - 1, 2 * s + 1, finish)

        @pl.when(s == late)
        def _():
            each_chunk(
                lambda ch: each_block(0, 2 * late - 1, lambda b: attend(b, ch, False, True))
            )
            each_block(0, 2 * late - 1, finish)

        return carry

    lax.fori_loop(late, n, step, 0)

    def middle(b, carry):
        project(b)
        return carry

    lax.fori_loop(1, n - 1, middle, 0)

    def ends(i, carry):
        project(jnp.where(2 * z < n, 1 - i, i) * (n - 1))
        return carry

    lax.fori_loop(0, 2, ends, 0)

    for offset in range(1, nx):
        for ch in range(chunks):
            xq_copy(offset, ch).wait_send()
        for kind in range(2):
            xkv_copy(offset, kind).wait_send()

    def sent(b, carry):
        for piece in range(nx):
            for ch in range(chunks):

                @pl.when((z < n - 1) & (b <= z))
                def _():
                    z_copy(0, b, piece, ch).wait_send()

                @pl.when((z > 0) & (b >= z))
                def _():
                    z_copy(1, b, piece, ch).wait_send()

        for offset in range(1, n):
            lse_copy(b, offset).wait_send()
        return carry

    lax.fori_loop(0, n, sent, 0)

    def collect(offset, carry):
        source = (me + offset) % members
        pltpu.make_async_remote_copy(
            src_ref=slab.at[source],
            dst_ref=landed.at[source],
            send_sem=v_send.at[source],
            recv_sem=v_recv.at[source],
            device_id=coords(source),
            device_id_type=MESH,
        ).wait()
        return carry

    lax.fori_loop(1, members, collect, 0)

    guided = jnp.sum(landed[:, pl.ds(0, half), :], axis=0)
    now = jnp.full((half, HD), step_ref[0], jnp.int32)
    sig_now = sigma_of(now.astype(F32))
    sig_next = sigma_of((now + 1).astype(F32))
    delta_ref[0] = (sig_next - sig_now) * guided
    delta_ref[1] = sig_now * guided


def on_device(
    n,
    nx,
    nc,
    queries,
    keys,
    values,
    ref_keys,
    ref_values,
    ref_len,
    step_index,
    guide,
    latent,
    w_out,
):
    rows, wide = queries.shape[1:]
    refs = ref_keys.shape[1]
    width = wide // nx
    heads = width // HD
    block = nx * rows
    padded = round_up(block, HD)
    stats = round_up(2 * heads, 8)
    members = n * nx * nc
    half = latent.shape[0]
    chunks = 4 if heads % 4 == 0 and heads > 4 else 1
    smem = pl.BlockSpec(memory_space=pltpu.SMEM)
    vmem = pl.BlockSpec(memory_space=pltpu.VMEM)
    anywhere = pl.BlockSpec(memory_space=pl.ANY)
    dma = pltpu.SemaphoreType.DMA
    flops = 4 * n * block * heads * HD * (refs + block)
    delta = pl.pallas_call(
        functools.partial(step_kernel, n, nx, nc, chunks),
        out_shape=jax.ShapeDtypeStruct((2,) + latent.shape, F32),
        in_specs=[smem] * 3 + [anywhere] * 6,
        out_specs=vmem,
        scratch_shapes=[
            pltpu.VMEM((n, nx, rows, width), BF16),
            pltpu.VMEM((nx, rows, width), BF16),
            pltpu.VMEM((nx, rows, width), BF16),
            pltpu.VMEM((refs, width), BF16),
            pltpu.VMEM((refs, width), BF16),
            pltpu.VMEM((2 * w_out.shape[1], width), BF16),
            pltpu.VMEM((block, width), BF16),
            pltpu.VMEM((refs, block), F32),
            pltpu.VMEM((heads, HD + ONES, refs), BF16),
            pltpu.VMEM((heads, HD + ONES, block), BF16),
            pltpu.VMEM((n, heads, HD, block), F32),
            pltpu.VMEM((n, heads, HD, block), F32),
            pltpu.VMEM((n, stats, block), F32),
            pltpu.VMEM((n, stats, block), F32),
            pltpu.VMEM((n, n, stats, block), F32),
            pltpu.VMEM((width, block), BF16),
            pltpu.VMEM((HD, padded), F32),
            pltpu.VMEM((padded, HD), F32),
            pltpu.VMEM((members, round_up(half, 8), HD), F32),
            pltpu.VMEM((members, round_up(half, 8), HD), F32),
            dma((7,)),
            dma((nx, chunks)),
            dma((2, nx)),
            dma((n, nx, chunks)),
            dma((2, nx)),
            dma((2, n, nx, chunks)),
            dma((n, n)),
            dma((n, n)),
            dma((members,)),
            dma((members,)),
        ],
        compiler_params=pltpu.CompilerParams(
            collective_id=0, has_side_effects=True, vmem_limit_bytes=58 * 2**20
        ),
        cost_estimate=pl.CostEstimate(
            flops=flops, bytes_accessed=4 * refs * width * 2, transcendentals=0
        ),
    )(ref_len, step_index, guide, queries, keys, values, ref_keys, ref_values, w_out.T)
    return latent + delta[0], latent - delta[1]


def solution(mesh):
    in_specs = (
        P(("groups", "cfg"), ("seq", "blk"), None),
        P(("groups", "cfg"), ("seq", "blk"), None),
        P(("groups", "cfg"), ("seq", "blk"), None),
        P(("groups", "cfg"), "seq", None),
        P(("groups", "cfg"), "seq", None),
        P(("groups", "cfg")),
        P("groups"),
        P("groups"),
        P(("groups", "seq", "blk", "cfg"), None),
        P(),
    )
    out_specs = (P(("groups", "seq", "blk", "cfg"), None), P(("groups", "seq", "blk", "cfg"), None))
    body = functools.partial(on_device, mesh.shape["seq"], mesh.shape["blk"], mesh.shape["cfg"])
    return jax.shard_map(
        body, mesh=mesh, in_specs=in_specs, out_specs=out_specs, check_vma=False
    )
```
